256 devices in a mesh: region: 8 (over x, core), sub: 32 (over z, y).
Axes of the slice: x: 4, y: 4, z: 8, core: 2. Of those that a mesh axis runs over, the one named last changes fastest.
Arguments:
- features: bfloat16 [1048576, 128], P(('region', 'sub')), may hold values from -6 to 6
- face_rows: int32 [512, 256], P(('region', 'sub')), may hold values from 0 to 4095
- sub_send: int32 [8192, 64], P(('region', 'sub')), may hold values from 0 to 4608, as said below
- neighbors: int32 [1048576, 27], P(('region', 'sub')), may hold values from 0 to 6656, as said below
- w_sub: bfloat16 [3456, 128], replicated, may hold values from -0.15625 to 0.15625
- parent_position: int32 [1048576], P(('region', 'sub')), may hold values from 0 to 7
- coarse_target: int32 [1048576], P(('region', 'sub')), may hold values from 0 to 16383, as said below
- w_down: bfloat16 [1024, 128], replicated, may hold values from -0.5 to 0.5
Outputs:
- fine: bfloat16 [1048576, 128], P(('region', 'sub'))
- coarse: bfloat16 [131072, 128], P(('region', 'sub'))
The draws below stay inside these ranges and needn't reach their ends.
Inputs may be any that keep to these rules, and one draw needn't show every extreme that they name: `sub_send`: toward each index of sub a device lists its live rows first and 4608 after them; nothing toward itself; toward the next index of sub, wrapping, all 64 slots are live. `neighbors`: rows of received blocks are only live slots; offset 27 // 2 is the voxel itself. `coarse_target`: at most 157 rows of one device have targets owned by any one other index of sub (target // 512); every device reaches it.
All inputs are finite; a program needn't handle non-finite values.
Results may differ from the reference program's by a relative error of at most 0.0065.
Values may be sent and summed in bfloat16 or wider, within the bound.
A program may use at most 64 MiB of HBM per device.

```python
import jax
import jax.numpy as jnp
from jax import lax

FEATURE_WIDTH = 128
KVOL = 27
VOXELS_PER_UNIT = 4096
CV_DEV = 512
HALO = 256
CAP = 64
REGION_GROUPS = 8
SUB_REGIONS = 32
PAD = 4608
ACTIVE_VOXELS = 1048576
COARSE = 131072
DEVICES = 256


def send_counts(key):
    counts = jax.random.randint(jax.random.fold_in(key, 101), (REGION_GROUPS, SUB_REGIONS, SUB_REGIONS), CAP // 3, CAP + 1)
    sender = jnp.arange(SUB_REGIONS)[None, :, None]
    target = jnp.arange(SUB_REGIONS)[None, None, :]
    counts = jnp.where(target == (sender + 1) % SUB_REGIONS, CAP, counts)
    counts = jnp.where(target == sender, 0, counts)
    return counts.astype(jnp.int32)


def draw_sub_send(key, part):
    counts = send_counts(key)
    key = jax.random.fold_in(key, 3)
    chosen = jax.random.randint(key, (REGION_GROUPS, SUB_REGIONS, SUB_REGIONS, CAP), 0, PAD)
    position = jnp.arange(CAP)[None, None, None, :]
    live_slot = position < counts[..., None]
    return jnp.where(live_slot, chosen, PAD).reshape(DEVICES * SUB_REGIONS, CAP).astype(jnp.int32)


def draw_neighbors(key, part):
    counts = send_counts(key)
    key = jax.random.fold_in(key, 5)
    key_kind, key_own, key_halo, key_peer, key_slot = jax.random.split(key, 5)
    shape = (REGION_GROUPS, SUB_REGIONS, VOXELS_PER_UNIT, KVOL)
    kinds = jax.random.randint(key_kind, shape, 0, 100)
    own_pick = jax.random.randint(key_own, shape, 0, VOXELS_PER_UNIT)
    halo_pick = jax.random.randint(key_halo, shape, 0, HALO)
    peer_pick = jax.random.randint(key_peer, shape, 0, SUB_REGIONS)
    region_grid = jnp.arange(REGION_GROUPS)[:, None, None, None]
    self_grid = jnp.arange(SUB_REGIONS)[None, :, None, None]
    live_count = counts[region_grid, peer_pick, self_grid]
    slot_pick = jax.random.randint(key_slot, shape, 0, CAP) % jnp.maximum(live_count, 1)
    received = PAD + 1 + peer_pick * CAP + slot_pick
    received = jnp.where(live_count > 0, received, PAD)
    chosen = jnp.where(kinds < 30, PAD, jnp.where(kinds < 75, own_pick, jnp.where(kinds < 82, VOXELS_PER_UNIT + halo_pick, jnp.where(kinds < 89, VOXELS_PER_UNIT + HALO + halo_pick, received))))
    centre = jnp.broadcast_to(jnp.arange(VOXELS_PER_UNIT)[None, None, :], (REGION_GROUPS, SUB_REGIONS, VOXELS_PER_UNIT))
    chosen = chosen.at[:, :, :, KVOL // 2].set(centre)
    upper_peer = (jnp.arange(SUB_REGIONS) - 1) % SUB_REGIONS
    last_slot = PAD + 1 + upper_peer * CAP + CAP - 1
    chosen = chosen.at[:, :, 0, 0].set(jnp.broadcast_to(last_slot[None, :], (REGION_GROUPS, SUB_REGIONS)))
    chosen = chosen.at[:, :, 0, 1].set(0)
    return chosen.reshape(ACTIVE_VOXELS, KVOL).astype(jnp.int32)


def draw_coarse_target(key, part):
    key = jax.random.fold_in(key, 11)
    key_order, key_slot = jax.random.split(key)
    device_keys = jax.random.split(key_order, DEVICES)
    ranking = jax.vmap(lambda single: jax.random.permutation(single, VOXELS_PER_UNIT))(device_keys)
    remote_count = VOXELS_PER_UNIT // 4
    skewed_count = VOXELS_PER_UNIT // 32
    later = ranking - (VOXELS_PER_UNIT - remote_count)
    self_index = (jnp.arange(DEVICES) % SUB_REGIONS)[:, None]
    heavy_step = 1 + self_index % (SUB_REGIONS - 1)
    cycled_step = 1 + (later - skewed_count + self_index) % (SUB_REGIONS - 1)
    step_away = jnp.where(later < skewed_count, heavy_step, cycled_step)
    owner = jnp.where(ranking < VOXELS_PER_UNIT - remote_count, self_index, (self_index + step_away) % SUB_REGIONS)
    within = jax.random.randint(key_slot, (DEVICES, VOXELS_PER_UNIT), 0, CV_DEV)
    return (owner * CV_DEV + within).reshape(ACTIVE_VOXELS).astype(jnp.int32)


def place_ends(result, key, low, largest):
    longest = result.shape.index(max(result.shape))
    spots = []
    for shift in (0, 1):
        where = [jax.random.randint(jax.random.fold_in(key, axis), (), 0, length) for axis, length in enumerate(result.shape)]
        where[longest] = (where[longest] + shift) % result.shape[longest]
        spots.append(tuple(where))
    return result.at[spots[0]].set(low).at[spots[1]].set(largest)


def level_of(stream_key, extent, shards, low, top_value):
    def one(axis_at, shards_of):
        draws = jax.random.uniform(jax.random.fold_in(jax.random.fold_in(stream_key, 6), axis_at), (shards_of,), jnp.float32, low / len(shards), top_value / len(shards))
        return jnp.repeat(jnp.exp(draws), extent[axis_at] // shards_of).reshape((-1,) + (1,) * (len(extent) - axis_at - 1))

    level = one(*shards[0])
    for cut in shards[1:]:
        level = level * one(*cut)
    return level


def noise(rng, dims, width, reach, shards=(), held_as=jnp.bfloat16):
    entries = width * jax.random.normal(rng, dims, jnp.float32)
    if shards:
        entries = entries * level_of(rng, dims, shards, -0.22, 0.18)
    return jnp.clip(entries, -reach, reach).astype(held_as)


def setup_inputs(seed: int = 0) -> dict:
    key_of = jax.random.split(jax.random.key(seed), 9)
    return {
        "features": noise(key_of[0], (ACTIVE_VOXELS, FEATURE_WIDTH), 1.0, 6.0, ((0, 256),)),
        "face_rows": place_ends(jax.random.randint(key_of[1], (2 * DEVICES, HALO), 0, VOXELS_PER_UNIT), jax.random.fold_in(key_of[1], 1), 0, VOXELS_PER_UNIT - 1).astype(jnp.int32),
        "sub_send": draw_sub_send(jax.random.fold_in(key_of[8], 71), 0),
        "neighbors": draw_neighbors(jax.random.fold_in(key_of[8], 71), 0),
        "w_sub": noise(key_of[4], (KVOL * FEATURE_WIDTH, FEATURE_WIDTH), (12 * FEATURE_WIDTH) ** -0.5, 0.15625),
        "parent_position": place_ends(jax.random.randint(key_of[5], (ACTIVE_VOXELS,), 0, 8), jax.random.fold_in(key_of[5], 1), 0, 7).astype(jnp.int32),
        "coarse_target": draw_coarse_target(jax.random.fold_in(key_of[8], 71), 0),
        "w_down": noise(key_of[7], (8 * FEATURE_WIDTH, FEATURE_WIDTH), FEATURE_WIDTH ** -0.5, 0.5),
    }


def pick_rows(table_one, index_one):
    return table_one[index_one]


def reference(features, face_rows, sub_send, neighbors, w_sub, parent_position, coarse_target, w_down):
    feats = features.reshape(REGION_GROUPS, SUB_REGIONS, VOXELS_PER_UNIT, FEATURE_WIDTH)
    faces = face_rows.reshape(REGION_GROUPS, SUB_REGIONS, 2, HALO)
    nested = jax.vmap(jax.vmap(pick_rows))
    sent_low = nested(feats, faces[:, :, 0])
    sent_high = nested(feats, faces[:, :, 1])
    zero_plane = jnp.zeros((1, SUB_REGIONS, HALO, FEATURE_WIDTH), jnp.bfloat16)
    from_below = jnp.concatenate([zero_plane, sent_high[:-1]], 0)
    from_above = jnp.concatenate([sent_low[1:], zero_plane], 0)
    blank_rows = jnp.zeros((REGION_GROUPS, SUB_REGIONS, 1, FEATURE_WIDTH), jnp.bfloat16)
    table = jnp.concatenate([feats, from_below, from_above, blank_rows], 2)
    plan = sub_send.reshape(REGION_GROUPS, SUB_REGIONS, SUB_REGIONS, CAP)
    outgoing = nested(table, plan)
    incoming = jnp.transpose(outgoing, (0, 2, 1, 3, 4)).reshape(REGION_GROUPS, SUB_REGIONS, SUB_REGIONS * CAP, FEATURE_WIDTH)
    full_table = jnp.concatenate([table, incoming], 2).reshape(REGION_GROUPS * SUB_REGIONS, -1, FEATURE_WIDTH)
    kernel_maps = neighbors.reshape(REGION_GROUPS * SUB_REGIONS, VOXELS_PER_UNIT, KVOL)
    own_rows = features.reshape(REGION_GROUPS * SUB_REGIONS, VOXELS_PER_UNIT, FEATURE_WIDTH)

    def convolve(argument_list):
        table_one, map_one, input_one = argument_list
        gathered = table_one[map_one].reshape(VOXELS_PER_UNIT, KVOL * FEATURE_WIDTH)
        summed = jnp.dot(gathered, w_sub, preferred_element_type=jnp.float32)
        return jax.nn.relu(input_one.astype(jnp.float32) + summed).astype(jnp.bfloat16)

    fine = lax.map(convolve, (full_table, kernel_maps, own_rows)).reshape(ACTIVE_VOXELS, FEATURE_WIDTH)

    def reduce_resolution(argument_list):
        fine_one, offset_one = argument_list
        chosen = offset_one[:, None, None] == jnp.arange(8, dtype=jnp.int32)[None, :, None]
        expanded = jnp.where(chosen, fine_one[:, None, :], jnp.zeros((), jnp.bfloat16)).reshape(VOXELS_PER_UNIT, 8 * FEATURE_WIDTH)
        return jnp.dot(expanded, w_down, preferred_element_type=jnp.float32)

    partial_result = lax.map(reduce_resolution, (fine.reshape(REGION_GROUPS * SUB_REGIONS, VOXELS_PER_UNIT, FEATURE_WIDTH), parent_position.reshape(REGION_GROUPS * SUB_REGIONS, VOXELS_PER_UNIT))).reshape(ACTIVE_VOXELS, FEATURE_WIDTH)
    group_base = (jnp.arange(ACTIVE_VOXELS, dtype=jnp.int32) // (SUB_REGIONS * VOXELS_PER_UNIT)) * (SUB_REGIONS * CV_DEV)
    coarse_ids = (group_base + coarse_target).astype(jnp.int32)
    coarse = jnp.zeros((COARSE, FEATURE_WIDTH), jnp.float32).at[coarse_ids].add(partial_result)
    return fine, coarse.astype(jnp.bfloat16)
```

```python
import functools

import jax
import jax.numpy as jnp
from jax import lax
from jax.experimental import pallas as pl
from jax.experimental.pallas import tpu as pltpu
from jax.sharding import PartitionSpec as P

F32, BF16, I32 = jnp.float32, jnp.bfloat16, jnp.int32
MESH = pl.DeviceIdType.MESH

WIDTH = 128
VOX = 4096
KVOL = 27
HALO = 256
PAD = VOX + 2 * HALO
RECV = PAD + 8
SUBS = 32
REGIONS = 8
CAP = 64
ROWS = RECV + SUBS * CAP
CV = VOX // 8
LANES = 128
BLOCK = 128
GROUP = 16
PARTS = ((0, 32), (32, 64), (64, 96), (96, 112), (112, 128), (128, 160))
AFTER = (9, 17, 25, 29, 32)
DEAD = VOX
NT = (((1,), (1,)), ((), ()))


def iota(shape, axis):
    return lax.broadcasted_iota(I32, shape, axis)


def exclusive_counts(onehot, upper):
    pieces, carry = [], jnp.zeros((onehot.shape[0], 1), F32)
    for start in range(0, VOX, 256):
        piece = onehot[:, start : start + 256]
        pieces.append(jnp.dot(piece, upper, preferred_element_type=F32) + carry)
        carry = carry + jnp.sum(piece.astype(F32), 1, keepdims=True)
    return jnp.concatenate(pieces, 1), carry


def plan_kernel(
    me_ref, target_ref, parent_ref, base_ref, local_ref, parent_out, place_ref,
    near_ref, far_ref, ids_ref,
):
    me = me_ref[0]
    target = target_ref[...]
    owner, within = target >> 9, target & (CV - 1)
    upper = (iota((256, 256), 0) < iota((256, 256), 1)).astype(F32).astype(BF16)
    owned = jnp.where(iota((SUBS, VOX), 0) == owner, 1.0, 0.0)
    before, _ = exclusive_counts(owned.astype(BF16), upper)
    rank = jnp.sum(owned * before, 0, keepdims=True).astype(I32)
    remote = owner != me
    part = sum((rank >= first).astype(I32) for first, _ in PARTS) - 1
    part = jnp.where(remote, part, len(PARTS))
    parts = jnp.where(iota((8, VOX), 0) == part, 1.0, 0.0)
    before, totals = exclusive_counts(parts.astype(BF16), upper)
    place = jnp.sum(
        parts * before + jnp.where(iota((8, VOX), 0) < part, totals, 0.0), 0, keepdims=True
    ).astype(I32)
    place_ref[...] = place

    def scatter(rows, values, lanes):
        stacked = jnp.concatenate([rows * v.astype(F32) for v in values], 0).astype(BF16)
        return lax.dot_general(stacked, lanes, NT, preferred_element_type=F32).astype(I32)

    voxel = iota((1, VOX), 1)
    near_id = jnp.where(remote, 0, within + 1)
    lanes = jnp.where(iota((LANES, VOX), 0) == (place & 127), 1.0, 0.0).astype(BF16)
    rows = jnp.where(iota((SUBS, VOX), 0) == (place >> 7), 1.0, 0.0)
    found = scatter(
        rows, [voxel >> 6, voxel & 63, near_id >> 5, near_id & 31, parent_ref[...]], lanes
    )
    order = found[0:32] * 64 + found[32:64]
    base_ref[...] = (order >> 7) * 1024 + (order & 127)
    local_ref[...] = found[64:96] * 32 + found[96:128]
    parent_out[...] = found[128:160].astype(F32)

    sent = jnp.where(remote, owned, 0.0)
    there = within + 1
    values = [place >> 6, place & 63, there >> 5, there & 31, jnp.ones((1, VOX), I32)]
    shifted = jnp.where(rank >= LANES, rank - LANES + 32 * (me % 4), -1)
    for which, (lane, out) in enumerate(((rank, near_ref), (shifted, far_ref))):
        lanes = jnp.where(iota((LANES, VOX), 0) == lane, 1.0, 0.0).astype(BF16)
        found = scatter(sent, values, lanes)
        out[...] = jnp.where(found[128:160] > 0, found[0:32] * 64 + found[32:64], DEAD)
        ids_ref[:, which, :] = found[64:96] * 32 + found[96:128]


def plan(me, coarse_target, parent_position):
    square = jax.ShapeDtypeStruct((SUBS, LANES), I32)
    vmem = pl.BlockSpec(memory_space=pltpu.VMEM)
    return pl.pallas_call(
        plan_kernel,
        out_shape=(
            square, square, jax.ShapeDtypeStruct((SUBS, LANES), F32),
            jax.ShapeDtypeStruct((1, VOX), I32), square, square,
            jax.ShapeDtypeStruct((SUBS, 2, LANES), I32),
        ),
        in_specs=[pl.BlockSpec(memory_space=pltpu.SMEM), vmem, vmem],
        out_specs=(vmem,) * 7,
        compiler_params=pltpu.CompilerParams(vmem_limit_bytes=48 << 20),
        name="plan",
    )(me.reshape(1), coarse_target.reshape(1, VOX), parent_position.reshape(1, VOX))


def pull(count, read, table, stage):
    for r in range(count):
        stage[r : r + 1, :] = table[pl.ds(read(r), 1), :]


def main_kernel(
    feat_hbm, face_hbm, send_hbm, maps_hbm, base_hbm, place_hbm, near_hbm, far_hbm,
    local, parent, ids, w_sub, w_down,
    fine_out, coarse_out,
    feat, face, send, maps, base, place, near, far,
    table, stage, held, sums, fine_rows, down_rows,
    halo_out, halo_in, list_out, list_in, ids_in, near_out, near_in, far_out, far_in, total,
    load_sem, halo_send, halo_recv, list_send, list_recv, ids_send, ids_recv, part_send, part_recv,
):
    region, me = lax.axis_index("region"), lax.axis_index("sub")
    below, above = lax.rem(region + REGIONS - 1, REGIONS), lax.rem(region + 1, REGIONS)
    loads = [
        pltpu.make_async_copy(source, landing, load_sem.at[i])
        for i, (source, landing) in enumerate(
            (
                (feat_hbm, feat), (face_hbm, face), (send_hbm, send), (maps_hbm, maps),
                (base_hbm, base), (place_hbm, place), (near_hbm, near), (far_hbm, far),
            )
        )
    ]
    for load in loads:
        load.start()

    barrier = pltpu.get_barrier_semaphore()
    pl.semaphore_signal(barrier, inc=1, device_id=(below, me), device_id_type=MESH)
    pl.semaphore_signal(barrier, inc=1, device_id=(above, me), device_id_type=MESH)

    def greet(d, c):
        peer = lax.rem(me + d, SUBS)
        pl.semaphore_signal(barrier, inc=1, device_id=(region, peer), device_id_type=MESH)
        return c

    lax.fori_loop(1, SUBS, greet, 0)
    table[PAD : PAD + 8, :] = jnp.zeros((8, WIDTH), F32)
    loads[0].wait()

    def widen(t, c):
        rows = pl.ds(pl.multiple_of(t * 64, 64), 64)
        table[rows, :] = feat[rows, :].astype(F32)
        return c

    lax.fori_loop(0, VOX // 64, widen, 0)
    loads[1].wait()

    def pull_face(t, c):
        pull(64, lambda r: face[t // 4, (t % 4) * 64 + r], table, stage)
        halo_out[pl.ds(pl.multiple_of(t * 64, 64), 64), :] = stage[...].astype(BF16)
        return c

    lax.fori_loop(0, 2 * HALO // 64, pull_face, 0)
    pl.semaphore_wait(barrier, SUBS + 1)

    halos = []
    for which, target in ((0, below), (1, above)):
        copy = pltpu.make_async_remote_copy(
            src_ref=halo_out.at[pl.ds(which * HALO, HALO)],
            dst_ref=halo_in.at[pl.ds((1 - which) * HALO, HALO)],
            send_sem=halo_send.at[which],
            recv_sem=halo_recv.at[which],
            device_id=(target, me),
            device_id_type=MESH,
        )
        copy.start()
        halos.append(copy)

    loads[2].wait()
    for copy in halos:
        copy.wait()
    exists_below = jnp.where(region > 0, 1.0, 0.0)
    exists_above = jnp.where(region < REGIONS - 1, 1.0, 0.0)
    table[VOX : VOX + HALO, :] = halo_in[0:HALO, :].astype(F32) * exists_below
    table[VOX + HALO : PAD, :] = halo_in[HALO:, :].astype(F32) * exists_above

    def send_list(d, c):
        peer = lax.rem(me + d, SUBS)
        pull(CAP, lambda r: send[peer, r], table, stage)
        list_out[peer] = stage[...].astype(BF16)
        pltpu.make_async_remote_copy(
            src_ref=list_out.at[peer], dst_ref=list_in.at[me],
            send_sem=list_send, recv_sem=list_recv,
            device_id=(region, peer), device_id_type=MESH,
        ).start()
        return c

    lax.fori_loop(1, SUBS, send_list, 0)

    near_in[me] = jnp.zeros((LANES, WIDTH), BF16)
    far_in[me] = jnp.zeros((32, WIDTH), BF16)
    total[...] = jnp.zeros((CV, WIDTH), F32)
    down_rows[VOX : VOX + 8, :] = jnp.zeros((8, WIDTH), F32)
    sums[...] = jnp.zeros((BLOCK, WIDTH), F32)
    for load in loads[3:]:
        load.wait()

    def settle(ref, sem):
        pltpu.make_async_copy(ref, ref, sem).wait()

    others = pl.ds(0, SUBS - 1)
    settle(list_in.at[others], list_recv)
    list_in[me] = jnp.zeros((CAP, WIDTH), BF16)

    def place_list(s, c):
        table[pl.ds(pl.multiple_of(RECV + s * CAP, 8), CAP), :] = list_in[s].astype(F32)
        return c

    lax.fori_loop(0, SUBS, place_list, 0)

    def send_ids(d, c):
        peer = lax.rem(me + d, SUBS)
        pltpu.make_async_remote_copy(
            src_ref=ids.at[peer], dst_ref=ids_in.at[me],
            send_sem=ids_send, recv_sem=ids_recv,
            device_id=(region, peer), device_id_type=MESH,
        ).start()
        return c

    lax.fori_loop(1, SUBS, send_ids, 0)

    def project(b):
        rows = pl.ds(pl.multiple_of(b * BLOCK, BLOCK), BLOCK)
        fine = jnp.maximum(sums[...], 0.0).astype(BF16).astype(F32)
        fine_rows[rows, :] = fine
        parents = jnp.broadcast_to(parent[pl.ds(b, 1), :], (BLOCK, LANES)).T
        spread = jnp.concatenate(
            [jnp.where(parents == p, fine, 0.0).astype(BF16) for p in range(8)], 1
        )
        down_rows[rows, :] = jnp.dot(spread, w_down[...], preferred_element_type=F32)

    def convolve(b, c):
        def gather(t, c):
            for q in range(GROUP // 8):
                for r in range(8):
                    at = base[b * BLOCK + t * GROUP + q * 8 + r]
                    for k in range(KVOL):
                        row = maps.at[pl.ds(at + ((k // 8) * 32768 + (k % 8) * LANES), 1)][0]
                        held[t * (GROUP // 8) + q, k, r : r + 1, :] = table[pl.ds(row, 1), :]
            return c

        lax.fori_loop(0, BLOCK // GROUP, gather, 0)
        project(jnp.maximum(b - 1, 0))
        wide = jnp.concatenate(
            [held[:, k].reshape(BLOCK, WIDTH).astype(BF16) for k in range(KVOL)], 1
        )
        own = held[:, KVOL // 2].reshape(BLOCK, WIDTH)
        sums[...] = own + jnp.dot(wide, w_sub[...], preferred_element_type=F32)
        return c

    def send_part(j):
        low, high = PARTS[j]
        count = high - low
        source, landing, first = (near_out, near_in, low) if high <= LANES else (far_out, far_in, 0)

        def one(d, c):
            peer = lax.rem(me + d, SUBS)
            if high <= LANES:
                pull(count, lambda r: near[peer * LANES + first + r], down_rows, stage)
            else:
                shift = 32 * lax.rem(me, 4)
                pull(count, lambda r: far[peer * LANES + shift + r], down_rows, stage)
            source[peer, first : first + count, :] = stage[0:count, :].astype(BF16)
            pltpu.make_async_remote_copy(
                src_ref=source.at[peer, pl.ds(first, count)],
                dst_ref=landing.at[me, pl.ds(first, count)],
                send_sem=part_send.at[j], recv_sem=part_recv.at[j],
                device_id=(region, peer), device_id_type=MESH,
            ).start()
            return c

        lax.fori_loop(1, SUBS, one, 0)

    start = 0
    for j, stop in enumerate(AFTER):
        lax.fori_loop(start, stop, convolve, 0)
        send_part(j)
        start = stop
    project(VOX // BLOCK - 1)
    send_part(5)

    def put_back(t, c):
        pull(64, lambda r: place[t * 64 + r], fine_rows, stage)
        fine_out[pl.ds(pl.multiple_of(t * 64, 64), 64), :] = stage[...].astype(BF16)
        return c

    lax.fori_loop(0, VOX // 64, put_back, 0)

    def accumulate(lane_ids, rows):
        hits = jnp.concatenate(
            [
                jnp.where(iota((CV, LANES), 0) + 1 == row, 1.0, 0.0).astype(BF16)
                for row in lane_ids
            ],
            1,
        )
        total[...] += jnp.dot(hits, rows, preferred_element_type=F32)

    def add_local(q, c):
        block = down_rows[pl.ds(pl.multiple_of(q * 1024, 1024), 1024), :].astype(BF16)
        eight = local[pl.ds(pl.multiple_of(q * 8, 8), 8), :]
        accumulate([eight[i : i + 1] for i in range(8)], block)
        return c

    lax.fori_loop(0, 4, add_local, 0)
    settle(ids_in.at[others], ids_recv)
    ids_in[me] = jnp.zeros((2, LANES), I32)
    for j, (low, high) in enumerate(PARTS[:-1]):
        settle(near_in.at[others, pl.ds(low, high - low)], part_recv.at[j])

    def add_near(q, c):
        block = near_in[pl.ds(q * 8, 8)].reshape(1024, WIDTH)
        accumulate([ids_in[q * 8 + i, 0:1, :] for i in range(8)], block)
        return c

    lax.fori_loop(0, 4, add_near, 0)
    settle(far_in.at[others], part_recv.at[5])
    lane_ids = [
        ids_in[4 * i, 1:2, :] + ids_in[4 * i + 1, 1:2, :]
        + ids_in[4 * i + 2, 1:2, :] + ids_in[4 * i + 3, 1:2, :]
        for i in range(8)
    ]
    accumulate(lane_ids, far_in[...].reshape(1024, WIDTH))
    coarse_out[...] = total[...].astype(BF16)
    settle(list_out.at[others], list_send)
    settle(ids.at[others], ids_send)
    for j, (low, high) in enumerate(PARTS[:-1]):
        settle(near_out.at[others, pl.ds(low, high - low)], part_send.at[j])
    settle(far_out.at[others], part_send.at[5])


def per_device(
    features, face_rows, sub_send, neighbors, w_sub, parent_position, coarse_target, w_down
):
    me = lax.axis_index("sub").astype(I32)
    base, local, parent, place, near, far, ids = plan(me, coarse_target, parent_position)
    moved = jnp.transpose(neighbors)
    moved = jnp.where(moved > PAD, moved + (RECV - PAD - 1), moved)
    maps = jnp.pad(moved, ((0, 32 - KVOL), (0, 0)))
    maps = maps.reshape(4, 8, VOX // LANES, LANES).transpose(0, 2, 1, 3).reshape(-1)
    vmem, anywhere = pl.BlockSpec(memory_space=pltpu.VMEM), pl.BlockSpec(memory_space=pl.ANY)
    dma = pltpu.SemaphoreType.DMA
    line = pltpu.SMEM((VOX,), I32)
    return pl.pallas_call(
        main_kernel,
        out_shape=(
            jax.ShapeDtypeStruct((VOX, WIDTH), BF16),
            jax.ShapeDtypeStruct((CV, WIDTH), BF16),
        ),
        in_specs=[anywhere] * 8 + [vmem] * 5,
        out_specs=(vmem, vmem),
        scratch_shapes=[
            pltpu.VMEM((VOX, WIDTH), BF16),
            pltpu.SMEM((2, HALO), I32),
            pltpu.SMEM((SUBS, CAP), I32),
            pltpu.SMEM((32 * VOX,), I32),
            line, line, line, line,
            pltpu.VMEM((ROWS, WIDTH), F32),
            pltpu.VMEM((64, WIDTH), F32),
            pltpu.VMEM((BLOCK // 8, KVOL, 8, WIDTH), F32),
            pltpu.VMEM((BLOCK, WIDTH), F32),
            pltpu.VMEM((VOX, WIDTH), F32),
            pltpu.VMEM((VOX + 8, WIDTH), F32),
            pltpu.VMEM((2 * HALO, WIDTH), BF16),
            pltpu.VMEM((2 * HALO, WIDTH), BF16),
            pltpu.VMEM((SUBS, CAP, WIDTH), BF16),
            pltpu.VMEM((SUBS, CAP, WIDTH), BF16),
            pltpu.VMEM((SUBS, 2, LANES), I32),
            pltpu.VMEM((SUBS, LANES, WIDTH), BF16),
            pltpu.VMEM((SUBS, LANES, WIDTH), BF16),
            pltpu.VMEM((SUBS, 32, WIDTH), BF16),
            pltpu.VMEM((SUBS, 32, WIDTH), BF16),
            pltpu.VMEM((CV, WIDTH), F32),
            dma((8,)), dma((2,)), dma((2,)), dma, dma, dma, dma, dma((6,)), dma((6,)),
        ],
        compiler_params=pltpu.CompilerParams(
            collective_id=0, has_side_effects=True, vmem_limit_bytes=48 << 20
        ),
        name="sparse_convolution",
    )(
        features, face_rows, sub_send, maps,
        base.reshape(-1), place.reshape(-1), near.reshape(-1), far.reshape(-1),
        local, parent, ids, w_sub, w_down,
    )


def solution(mesh):
    split, whole = P(("region", "sub"), None), P()
    line = P(("region", "sub"))
    return jax.shard_map(
        per_device,
        mesh=mesh,
        in_specs=(split, split, split, split, whole, line, line, whole),
        out_specs=(split, split),
        check_vma=False,
    )
```
